32 devices in a mesh: groups: 2 (over y), query: 4 (over z), proj: 4 (over x, core).
Axes of the slice: x: 2, y: 2, z: 4, core: 2. Of those that a mesh axis runs over, the one named last changes fastest.
Arguments:
- query_feats: float32 [4096, 8192], P(('groups', 'query'), 'proj'), parts along dimension 0, may hold values from -6 to 6
- train_feats: float32 [2048, 8192], P(('groups', 'query'), 'proj'), parts along dimension 0, may hold values from -0.0625 to 0.0625
- out_weight: float32 [2048], P(('groups', 'proj')), parts along dimension 0, may hold values from 0.05 to 1
Outputs:
- scores: float32 [2048, 2048], P(('groups', 'proj'), 'query'), parts along dimension 0
The draws below stay inside these ranges and needn't reach their ends.
There are 2 independent parts, one for each index of `groups`. The reference program is written for one: setup_inputs(seed, part) draws one part's arguments, and reference() takes and returns one part's arrays. A program takes and returns all parts, laid end to end along the dimension named above; each array names one. Nothing has to cross between parts.
All inputs are finite; a program needn't handle non-finite values.
Results may differ from the reference program's by a relative error of at most 0.000078.
Values sent between devices are 32-bit elements; how exact they have to be, the bound alone decides.
A program may use at most 128 MiB of HBM per device.

```python
import math
import jax
import jax.numpy as jnp
from jax import lax

K = 8192
QUERIES = 2048
TRAIN = 1024


def block_scale(stream_key, extent, pieces, low, largest):
    level, own = 1.0, jax.random.fold_in(stream_key, 6)
    for axis_at, shards_of in pieces:
        heights = jnp.exp(jax.random.uniform(jax.random.fold_in(own, axis_at), (shards_of,), jnp.float32, low / len(pieces), largest / len(pieces)))
        level = level * jnp.repeat(heights, extent[axis_at] // shards_of).reshape([-1 if axis == axis_at else 1 for axis in range(len(extent))])
    return level


def normal_values(own_key, shape, deviation, most, split=(), kind=jnp.bfloat16):
    values = jax.random.normal(own_key, shape, jnp.float32) * deviation
    if len(split) > 0:
        values = block_scale(own_key, shape, split, -0.22, 0.18) * values
    return jnp.clip(values, min=-most, max=most).astype(kind)


def setup_inputs(seed: int = 0, part: int = 0) -> dict:
    splits = jax.random.split(jax.random.key(seed), 4)
    part_splits = jax.random.split(jax.random.fold_in(splits[3], part), 4)
    query_feats = normal_values(part_splits[0], (QUERIES, K), 1.0, 6.0, ((0, 4), (1, 4)), jnp.float32)
    train_feats = normal_values(part_splits[1], (TRAIN, K), K ** -0.5, 0.0625, ((0, 4), (1, 4)), jnp.float32)
    out_weight = jnp.clip(jnp.exp(math.log(1.0) - 2.9957323 * jax.random.uniform(part_splits[2], (TRAIN,), jnp.float32) ** block_scale(part_splits[2], (TRAIN,), ((0, 4),), -0.2, 0.2)), 0.05, 1.0)
    return {"query_feats": query_feats, "train_feats": train_feats, "out_weight": out_weight}


def reference(query_feats, train_feats, out_weight):
    inner = lax.dot_general(train_feats, query_feats, (((1,), (1,)), ((), ())), precision=lax.Precision.HIGHEST, preferred_element_type=jnp.float32)
    return inner * out_weight[:, None]
```

```python
import functools
import jax
import jax.numpy as jnp
from jax import lax
from jax.sharding import PartitionSpec as P
import jax.experimental.pallas as pl
import jax.experimental.pallas.tpu as pltpu

MESH = pl.DeviceIdType.MESH
INWARD = 896
CHUNKS = 8


def split(values):
    high = values.astype(jnp.bfloat16)
    return high, (values - high.astype(jnp.float32)).astype(jnp.bfloat16)


def product(rows, high, low):
    dims = (((1,), (1,)), ((), ()))
    rows_high, rows_low = split(rows)
    count = rows.shape[0]
    first = lax.dot_general(
        jnp.concatenate([rows_high, rows_low], axis=0), high, dims, preferred_element_type=jnp.float32
    )
    second = lax.dot_general(rows_high, low, dims, preferred_element_type=jnp.float32)
    return first[:count] + (first[count:] + second)


def kernel(
    inward, chunks, q_ref, t_ref, o_ref,
    train, query, query_in, high, low, high_in, low_in, partial, taken, sums, sums_taken,
    local_sem, train_recv, query_recv, part_recv, sums_recv, in_send, out_send, query_send, part_send, sums_send,
):
    g, z, p = lax.axis_index("groups"), lax.axis_index("query"), lax.axis_index("proj")
    count = t_ref.shape[0] // chunks
    depth = t_ref.shape[1]
    queries = q_ref.shape[0]
    is_end = jnp.logical_or(z == 0, z == 3)
    is_mid = jnp.logical_not(is_end)
    beside = jnp.where(z == 0, 1, 2)
    across = 3 - z
    end = jnp.where(z == 1, 0, 3)
    far = 3 - end
    outer = pl.ds(inward, depth - inward)
    inner = pl.ds(0, inward)

    def rows_of(j):
        return pl.ds(pl.multiple_of(j * count, count), count)

    def send(src, dst, send_sem, recv_sem, to_z, to_p):
        return pltpu.make_async_remote_copy(
            src_ref=src, dst_ref=dst, send_sem=send_sem, recv_sem=recv_sem,
            device_id=(g, to_z, to_p), device_id_type=MESH,
        )

    def own_in(j, to_z):
        rows = rows_of(j)
        return send(t_ref.at[rows], train.at[z, rows], in_send.at[0, j], train_recv.at[z, j], to_z, p)

    def pass_in(j):
        rows = rows_of(j)
        return send(train.at[end, rows], train.at[end, rows], in_send.at[1, j], train_recv.at[end, j], across, p)

    def own_out(j):
        rows = rows_of(j)
        return send(t_ref.at[rows, outer], train.at[z, rows, outer], out_send.at[0, j], train_recv.at[z, j], end, p)

    def pass_out(j, block, k):
        part = train.at[block, rows_of(j), outer]
        return send(part, part, out_send.at[k, j], train_recv.at[block, j], end, p)

    def query_copy(to_z):
        return send(q_ref.at[:, inner], query_in, query_send.at[0], query_recv.at[0], to_z, p)

    def part_copy(j, half, block):
        rows = rows_of(j)
        return send(
            partial.at[half, block, rows], taken.at[p, half, rows],
            part_send.at[block, half, j], part_recv.at[p, half, j], z, block,
        )

    def part_wait(j, half, peer):
        dst = taken.at[peer, half, rows_of(j)]
        send(dst, dst, part_send.at[0, half, j], part_recv.at[peer, half, j], z, peer).wait_recv()

    def sums_copy(j, to_z):
        rows = rows_of(j)
        return send(sums.at[rows], sums_taken.at[rows], sums_send.at[j], sums_recv.at[j], to_z, p)

    def loop(body):
        def step(j, carry):
            body(j)
            return carry
        lax.fori_loop(0, chunks, step, 0)

    def send_parts(j, half, blocks):
        for block in blocks:
            @pl.when(p != block)
            def _():
                part_copy(j, half, block).start()

    def multiply(j, half, blocks, columns, by_high, by_low):
        rows = rows_of(j)
        result = product(
            jnp.concatenate([train[block, rows, columns] for block in blocks], axis=0), by_high, by_low
        )
        for k, block in enumerate(blocks):
            partial[half, block, rows] = result[k * count:(k + 1) * count]
        send_parts(j, half, blocks)

    def reduced(j, half):
        rows = rows_of(j)
        total = partial[half, p, rows]
        for step in range(1, 4):
            peer = lax.rem(p + step, 4)
            part_wait(j, half, peer)
            total = total + taken[peer, half, rows]
        return total

    own_train = pltpu.make_async_copy(t_ref, train.at[z], local_sem.at[0])
    own_query = pltpu.make_async_copy(q_ref, query, local_sem.at[1])
    own_train.start()
    own_query.start()

    barrier = pltpu.get_barrier_semaphore()
    for step in range(1, 4):
        pl.semaphore_signal(barrier, inc=1, device_id=(g, z, lax.rem(p + step, 4)), device_id_type=MESH)

    @pl.when(is_end)
    def _():
        pl.semaphore_signal(barrier, inc=1, device_id=(g, beside, p), device_id_type=MESH)
        pl.semaphore_wait(barrier, 4)

    @pl.when(is_mid)
    def _():
        pl.semaphore_signal(barrier, inc=1, device_id=(g, across, p), device_id_type=MESH)
        pl.semaphore_signal(barrier, inc=1, device_id=(g, end, p), device_id_type=MESH)
        pl.semaphore_wait(barrier, 5)

    @pl.when(is_end)
    def _():
        query_copy(beside).start()
        loop(lambda j: own_in(j, beside).start())

    @pl.when(is_mid)
    def _():
        def begin(j):
            own_in(j, across).start()
            own_out(j).start()
        loop(begin)

    own_train.wait()
    own_query.wait()

    def split_query(j):
        size = queries // chunks
        rows = pl.ds(pl.multiple_of(j * size, size), size)
        high[rows], low[rows] = split(query[rows])
    loop(split_query)

    @pl.when(is_mid)
    def _():
        def early(j):
            own_in_wait = send(
                train.at[across, rows_of(j)], train.at[across, rows_of(j)],
                in_send.at[0, j], train_recv.at[across, j], across, p,
            )
            own_in_wait.wait_recv()
            pass_out(j, across, 1).start()
            multiply(j, 0, (1, 2), slice(None), high[...], low[...])
        loop(early)

        def late(j):
            pass_in(j).wait_recv()
            pass_in(j).start()
            rows = rows_of(j)
            send(
                train.at[far, rows], train.at[far, rows], in_send.at[1, j], train_recv.at[far, j], across, p
            ).wait_recv()
            pass_out(j, far, 2).start()

            @pl.when(j == 0)
            def _():
                query_copy(end).wait_recv()

                def split_in(k):
                    size = queries // chunks
                    some = pl.ds(pl.multiple_of(k * size, size), size)
                    high_in[some], low_in[some] = split(query_in[some])
                loop(split_in)

            multiply(j, 1, (0, 1, 2, 3), slice(0, inward), high_in[...], low_in[...])
            multiply(j, 0, (0, 3), slice(None), high[...], low[...])

            @pl.when(j > 0)
            def _():
                finish(j - 1)

        def finish(j):
            rows = rows_of(j)
            sums[rows] = reduced(j, 1)
            sums_copy(j, end).start()
            o_ref[rows] = reduced(j, 0)

        loop(late)
        finish(chunks - 1)

        def drain(j):
            own_in(j, across).wait_send()
            pass_in(j).wait_send()
            own_out(j).wait_send()
            pass_out(j, across, 1).wait_send()
            pass_out(j, far, 2).wait_send()
            sums_copy(j, end).wait_send()
            for half in (0, 1):
                for block in range(4):
                    @pl.when(p != block)
                    def _():
                        part_copy(j, half, block).wait_send()
        loop(drain)

    @pl.when(is_end)
    def _():
        def wait_train(j, block):
            part = train.at[block, rows_of(j), outer]
            send(part, part, in_send.at[0, j], train_recv.at[block, j], beside, p).wait_recv()

        def early(j):
            wait_train(j, 1)
            wait_train(j, 2)
            multiply(j, 0, (1, 2), slice(inward, depth), high[:, inward:], low[:, inward:])
        loop(early)

        def late(j):
            wait_train(j, across)
            multiply(j, 0, (0, 3), slice(inward, depth), high[:, inward:], low[:, inward:])
        loop(late)

        def finish(j):
            rows = rows_of(j)
            total = reduced(j, 0)
            sums_copy(j, beside).wait_recv()
            o_ref[rows] = total + sums_taken[rows]
        loop(finish)

        query_copy(beside).wait_send()

        def drain(j):
            own_in(j, beside).wait_send()
            for block in range(4):
                @pl.when(p != block)
                def _():
                    part_copy(j, 0, block).wait_send()
        loop(drain)


def line_of_four(query_feats, train_feats, out_weight):
    queries, depth = query_feats.shape
    rows = train_feats.shape[0]
    inward = min(INWARD, depth // 2)
    f32, bf16 = jnp.float32, jnp.bfloat16
    dma = pltpu.SemaphoreType.DMA
    sums = pl.pallas_call(
        functools.partial(kernel, inward, CHUNKS),
        out_shape=jax.ShapeDtypeStruct((rows, queries), f32),
        in_specs=[pl.BlockSpec(memory_space=pl.ANY)] * 2,
        out_specs=pl.BlockSpec(memory_space=pltpu.VMEM),
        scratch_shapes=[
            pltpu.VMEM((4, rows, depth), f32),
            pltpu.VMEM((queries, depth), f32),
            pltpu.VMEM((queries, inward), f32),
            pltpu.VMEM((queries, depth), bf16),
            pltpu.VMEM((queries, depth), bf16),
            pltpu.VMEM((queries, inward), bf16),
            pltpu.VMEM((queries, inward), bf16),
            pltpu.VMEM((2, 4, rows, queries), f32),
            pltpu.VMEM((4, 2, rows, queries), f32),
            pltpu.VMEM((rows, queries), f32),
            pltpu.VMEM((rows, queries), f32),
            dma((2,)),
            dma((4, CHUNKS)),
            dma((1,)),
            dma((4, 2, CHUNKS)),
            dma((CHUNKS,)),
            dma((2, CHUNKS)),
            dma((3, CHUNKS)),
            dma((1,)),
            dma((4, 2, CHUNKS)),
            dma((CHUNKS,)),
        ],
        compiler_params=pltpu.CompilerParams(
            collective_id=0, has_side_effects=True, vmem_limit_bytes=56 << 20
        ),
        cost_estimate=pl.CostEstimate(
            flops=3 * 2 * 4 * rows * queries * depth, bytes_accessed=4 * (rows + queries) * depth, transcendentals=0
        ),
    )(query_feats, train_feats)
    return sums * out_weight[:, None]


def any_mesh(query_feats, train_feats, out_weight):
    terms = lax.dot_general(
        lax.all_gather(train_feats, "query", axis=0, tiled=True),
        query_feats,
        (((1,), (1,)), ((), ())),
        precision=lax.Precision.HIGHEST,
        preferred_element_type=jnp.float32,
    )
    return lax.psum_scatter(terms, "proj", scatter_dimension=0, tiled=True) * out_weight[:, None]


def solution(mesh):
    placed = (P(("groups", "query"), "proj"), P(("groups", "query"), "proj"), P(("groups", "proj")))
    body = line_of_four if mesh.shape["query"] == mesh.shape["proj"] == 4 else any_mesh
    return jax.shard_map(
        body, mesh=mesh, in_specs=placed, out_specs=P(("groups", "proj"), "query"), check_vma=False
    )
```

```python
import functools
import jax
import jax.numpy as jnp
from jax import lax
from jax.sharding import PartitionSpec as P
import jax.experimental.pallas as pl
import jax.experimental.pallas.tpu as pltpu

MESH = pl.DeviceIdType.MESH
INWARD = 768
CHUNKS = 16
GROUPS = 8


def split(values):
    high = values.astype(jnp.bfloat16)
    return high, (values - high.astype(jnp.float32)).astype(jnp.bfloat16)


def product(rows, high, low):
    dims = (((1,), (0,)), ((), ()))
    rows_high, rows_low = split(rows)
    count = rows.shape[0]
    first = lax.dot_general(
        jnp.concatenate([rows_high, rows_low], axis=0), high, dims, preferred_element_type=jnp.float32
    )
    second = lax.dot_general(rows_high, low, dims, preferred_element_type=jnp.float32)
    return first[:count] + (first[count:] + second)


def kernel(
    inward, chunks, groups, q_ref, t_ref, o_ref,
    train, query, query_in, high, low, high_in, low_in, partial, taken, sums, sums_taken,
    local_sem, train_recv, query_recv, part_recv, sums_recv, in_send, out_send, query_send, part_send, sums_send,
):
    g, z, p = lax.axis_index("groups"), lax.axis_index("query"), lax.axis_index("proj")
    count = t_ref.shape[0] // chunks
    depth = t_ref.shape[1]
    queries = q_ref.shape[0]
    is_end = jnp.logical_or(z == 0, z == 3)
    is_mid = jnp.logical_not(is_end)
    beside = jnp.where(z == 0, 1, 2)
    across = 3 - z
    end = jnp.where(z == 1, 0, 3)
    far = 3 - end
    outer = pl.ds(inward, depth - inward)
    inner = pl.ds(0, inward)

    def rows_of(j):
        return pl.ds(pl.multiple_of(j * count, count), count)

    def group_rows(s):
        size = t_ref.shape[0] // groups
        return pl.ds(pl.multiple_of(s * size, size), size)

    def send(src, dst, send_sem, recv_sem, to_z, to_p):
        return pltpu.make_async_remote_copy(
            src_ref=src, dst_ref=dst, send_sem=send_sem, recv_sem=recv_sem,
            device_id=(g, to_z, to_p), device_id_type=MESH,
        )

    def own_in(j, to_z):
        rows = rows_of(j)
        return send(t_ref.at[rows], train.at[z, rows], in_send.at[0, j], train_recv.at[z, j], to_z, p)

    def pass_in(j):
        rows = rows_of(j)
        return send(train.at[end, rows], train.at[end, rows], in_send.at[1, j], train_recv.at[end, j], across, p)

    def own_out(j):
        rows = rows_of(j)
        return send(t_ref.at[rows, outer], train.at[z, rows, outer], out_send.at[0, j], train_recv.at[z, j], end, p)

    def pass_out(j, block, k):
        part = train.at[block, rows_of(j), outer]
        return send(part, part, out_send.at[k, j], train_recv.at[block, j], end, p)

    def query_copy(to_z):
        return send(q_ref.at[:, inner], query_in, query_send.at[0], query_recv.at[0], to_z, p)

    def part_copy(j, half, block):
        rows = group_rows(j)
        return send(
            partial.at[half, block, rows], taken.at[p, half, rows],
            part_send.at[block, half, j], part_recv.at[p, half, j], z, block,
        )

    def part_wait(j, half, peer):
        dst = taken.at[peer, half, group_rows(j)]
        send(dst, dst, part_send.at[0, half, j], part_recv.at[peer, half, j], z, peer).wait_recv()

    def sums_copy(j, to_z):
        rows = group_rows(j)
        return send(sums.at[rows], sums_taken.at[rows], sums_send.at[j], sums_recv.at[j], to_z, p)

    def loop(body, low=0, high=chunks):
        def step(j, carry):
            body(j)
            return carry
        lax.fori_loop(low, high, step, 0)

    def multiply(first, number, half, blocks, columns, by_high, by_low):
        rows = pl.ds(pl.multiple_of(first, number), number)
        result = product(
            jnp.concatenate([train[block, rows, columns] for block in blocks], axis=0), by_high, by_low
        )
        for k, block in enumerate(blocks):
            partial[half, block, rows] = result[k * number:(k + 1) * number]

    def send_parts(s, half, block):
        @pl.when(p != block)
        def _():
            part_copy(s, half, block).start()

    def reduced(s, half):
        rows = group_rows(s)
        total = partial[half, p, rows]
        for step in range(1, 4):
            peer = lax.rem(p + step, 4)
            part_wait(s, half, peer)
            total = total + taken[peer, half, rows]
        return total

    def split_query(src, into_high, into_low):
        size = 128
        def step(k):
            some = pl.ds(pl.multiple_of(k * size, size), size)
            into_high[:, some], into_low[:, some] = split(src[some].T)
        loop(step, 0, queries // size)

    own_train = pltpu.make_async_copy(t_ref, train.at[z], local_sem.at[0])
    own_query = pltpu.make_async_copy(q_ref, query, local_sem.at[1])
    own_train.start()
    own_query.start()

    barrier = pltpu.get_barrier_semaphore()
    for step in range(1, 4):
        pl.semaphore_signal(barrier, inc=1, device_id=(g, z, lax.rem(p + step, 4)), device_id_type=MESH)

    @pl.when(is_end)
    def _():
        pl.semaphore_signal(barrier, inc=1, device_id=(g, beside, p), device_id_type=MESH)
        pl.semaphore_wait(barrier, 4)

    @pl.when(is_mid)
    def _():
        pl.semaphore_signal(barrier, inc=1, device_id=(g, across, p), device_id_type=MESH)
        pl.semaphore_signal(barrier, inc=1, device_id=(g, end, p), device_id_type=MESH)
        pl.semaphore_wait(barrier, 5)

    @pl.when(is_end)
    def _():
        query_copy(beside).start()
        loop(lambda j: own_in(j, beside).start())

    @pl.when(is_mid)
    def _():
        def begin(j):
            own_in(j, across).start()
            own_out(j).start()
        loop(begin)

    own_train.wait()
    own_query.wait()
    split_query(query, high, low)
    all_rows = t_ref.shape[0]
    per = chunks // groups
    size = all_rows // groups

    def send_all(half, block):
        loop(lambda s: send_parts(s, half, block), 0, groups)

    @pl.when(is_mid)
    def _():
        def wait_train(j, block):
            part = train.at[block, rows_of(j)]
            send(part, part, in_send.at[0, j], train_recv.at[block, j], across, p).wait_recv()

        def take_across(s):
            for k in range(per):
                wait_train(s * per + k, across)
                pass_out(s * per + k, across, 1).start()

        def take_end(s):
            for k in range(per):
                wait_train(s * per + k, end)
                pass_in(s * per + k).start()

        def take_far(s):
            for k in range(per):
                wait_train(s * per + k, far)
                pass_out(s * per + k, far, 2).start()

        def whole(s, block):
            multiply(s * size, size, 0, (block,), slice(None), high[...], low[...])
            send_parts(s, 0, block)

        def inward_part(s, block):
            multiply(s * size, size, 1, (block,), slice(0, inward), high_in[...], low_in[...])
            send_parts(s, 1, block)

        multiply(0, all_rows, 0, (z,), slice(None), high[...], low[...])
        send_all(0, z)

        def early(s):
            take_across(s)

            @pl.when(s == groups - 1)
            def _():
                take_end(0)

            whole(s, across)
        loop(early, 0, groups)

        query_copy(end).wait_recv()
        split_query(query_in, high_in, low_in)
        multiply(0, all_rows, 1, (1, 2), slice(0, inward), high_in[...], low_in[...])
        send_all(1, 1)
        send_all(1, 2)

        def finish(s):
            rows = group_rows(s)
            sums[rows] = reduced(s, 1)
            sums_copy(s, end).start()
            o_ref[rows] = reduced(s, 0)

        def late(s):
            @pl.when(s < groups - 1)
            def _():
                take_end(s + 1)

            def one(k):
                block = jnp.where(k == 0, end, far)

                @pl.when(k == 1)
                def _():
                    take_far(s)

                inward_part(s, block)
                whole(s, block)
            loop(one, 0, 2)

            @pl.when(s > 0)
            def _():
                finish(s - 1)
        loop(late, 0, groups)
        finish(groups - 1)

        def drain(j):
            own_in(j, across).wait_send()
            pass_in(j).wait_send()
            own_out(j).wait_send()
            pass_out(j, across, 1).wait_send()
            pass_out(j, far, 2).wait_send()
        loop(drain)

        def drain_parts(s):
            sums_copy(s, end).wait_send()
            for half in (0, 1):
                for block in range(4):
                    @pl.when(p != block)
                    def _():
                        part_copy(s, half, block).wait_send()
        loop(drain_parts, 0, groups)

    @pl.when(is_end)
    def _():
        columns = slice(inward, depth)

        def wait_train(s, block):
            for k in range(per):
                part = train.at[block, rows_of(s * per + k), outer]
                send(part, part, in_send.at[0, 0], train_recv.at[block, s * per + k], beside, p).wait_recv()

        multiply(0, all_rows, 0, (z,), columns, high[inward:], low[inward:])
        send_all(0, z)

        def early(s):
            wait_train(s, 1)
            wait_train(s, 2)
            multiply(s * size, size, 0, (1, 2), columns, high[inward:], low[inward:])
            send_parts(s, 0, 1)
            send_parts(s, 0, 2)
        loop(early, 0, groups)

        def late(s):
            wait_train(s, across)
            multiply(s * size, size, 0, (across,), columns, high[inward:], low[inward:])
            send_parts(s, 0, across)
        loop(late, 0, groups)

        def finish(s):
            rows = group_rows(s)
            o_ref[rows] = reduced(s, 0)
        loop(finish, 0, groups)

        def add_sums(s):
            rows = group_rows(s)
            sums_copy(s, beside).wait_recv()
            o_ref[rows] = o_ref[rows] + sums_taken[rows]
        loop(add_sums, 0, groups)

        query_copy(beside).wait_send()
        loop(lambda j: own_in(j, beside).wait_send())

        def drain_parts(s):
            for block in range(4):
                @pl.when(p != block)
                def _():
                    part_copy(s, 0, block).wait_send()
        loop(drain_parts, 0, groups)


def line_of_four(query_feats, train_feats, out_weight):
    queries, depth = query_feats.shape
    rows = train_feats.shape[0]
    inward = min(INWARD, depth // 2)
    f32, bf16 = jnp.float32, jnp.bfloat16
    dma = pltpu.SemaphoreType.DMA
    sums = pl.pallas_call(
        functools.partial(kernel, inward, CHUNKS, GROUPS),
        out_shape=jax.ShapeDtypeStruct((rows, queries), f32),
        in_specs=[pl.BlockSpec(memory_space=pl.ANY)] * 2,
        out_specs=pl.BlockSpec(memory_space=pltpu.VMEM),
        scratch_shapes=[
            pltpu.VMEM((4, rows, depth), f32),
            pltpu.VMEM((queries, depth), f32),
            pltpu.VMEM((queries, inward), f32),
            pltpu.VMEM((depth, queries), bf16),
            pltpu.VMEM((depth, queries), bf16),
            pltpu.VMEM((inward, queries), bf16),
            pltpu.VMEM((inward, queries), bf16),
            pltpu.VMEM((2, 4, rows, queries), f32),
            pltpu.VMEM((4, 2, rows, queries), f32),
            pltpu.VMEM((rows, queries), f32),
            pltpu.VMEM((rows, queries), f32),
            dma((2,)),
            dma((4, CHUNKS)),
            dma((1,)),
            dma((4, 2, GROUPS)),
            dma((GROUPS,)),
            dma((2, CHUNKS)),
            dma((3, CHUNKS)),
            dma((1,)),
            dma((4, 2, GROUPS)),
            dma((GROUPS,)),
        ],
        compiler_params=pltpu.CompilerParams(
            collective_id=0, has_side_effects=True, vmem_limit_bytes=56 << 20
        ),
        cost_estimate=pl.CostEstimate(
            flops=3 * 2 * 4 * rows * queries * depth, bytes_accessed=4 * (rows + queries) * depth, transcendentals=0
        ),
    )(query_feats, train_feats)
    return sums * out_weight[:, None]


def any_mesh(query_feats, train_feats, out_weight):
    terms = lax.dot_general(
        lax.all_gather(train_feats, "query", axis=0, tiled=True),
        query_feats,
        (((1,), (1,)), ((), ())),
        precision=lax.Precision.HIGHEST,
        preferred_element_type=jnp.float32,
    )
    return lax.psum_scatter(terms, "proj", scatter_dimension=0, tiled=True) * out_weight[:, None]


def solution(mesh):
    placed = (P(("groups", "query"), "proj"), P(("groups", "query"), "proj"), P(("groups", "proj")))
    body = line_of_four if mesh.shape["query"] == mesh.shape["proj"] == 4 else any_mesh
    return jax.shard_map(
        body, mesh=mesh, in_specs=placed, out_specs=P(("groups", "proj"), "query"), check_vma=False
    )
```

```python
import functools
import jax
import jax.numpy as jnp
from jax import lax
from jax.sharding import PartitionSpec as P
import jax.experimental.pallas as pl
import jax.experimental.pallas.tpu as pltpu

MESH = pl.DeviceIdType.MESH
INWARD = 768
CHUNKS = 16
GROUPS = 8


def split(values):
    high = values.astype(jnp.bfloat16)
    return high, (values - high.astype(jnp.float32)).astype(jnp.bfloat16)


def product(rows, high, low):
    dims = (((1,), (0,)), ((), ()))
    rows_high, rows_low = split(rows)
    count = rows.shape[0]
    first = lax.dot_general(
        jnp.concatenate([rows_high, rows_low], axis=0), high, dims, preferred_element_type=jnp.float32
    )
    second = lax.dot_general(rows_high, low, dims, preferred_element_type=jnp.float32)
    return first[:count] + (first[count:] + second)


def kernel(
    inward, chunks, groups, q_ref, t_ref, o_ref,
    train, query, query_in, high, low, high_in, low_in, partial, taken, sums, sums_taken,
    local_sem, train_recv, query_recv, part_recv, sums_recv, in_send, out_send, query_send, part_send, sums_send,
):
    g, z, p = lax.axis_index("groups"), lax.axis_index("query"), lax.axis_index("proj")
    count = t_ref.shape[0] // chunks
    depth = t_ref.shape[1]
    queries = q_ref.shape[0]
    is_end = jnp.logical_or(z == 0, z == 3)
    is_mid = jnp.logical_not(is_end)
    beside = jnp.where(z == 0, 1, 2)
    across = 3 - z
    end = jnp.where(z == 1, 0, 3)
    far = 3 - end
    outer = pl.ds(inward, depth - inward)
    inner = pl.ds(0, inward)

    def rows_of(j):
        return pl.ds(pl.multiple_of(j * count, count), count)

    def group_rows(s):
        size = t_ref.shape[0] // groups
        return pl.ds(pl.multiple_of(s * size, size), size)

    def send(src, dst, send_sem, recv_sem, to_z, to_p):
        return pltpu.make_async_remote_copy(
            src_ref=src, dst_ref=dst, send_sem=send_sem, recv_sem=recv_sem,
            device_id=(g, to_z, to_p), device_id_type=MESH,
        )

    def own_in(j, to_z):
        rows = rows_of(j)
        return send(t_ref.at[rows], train.at[z, rows], in_send.at[0, j], train_recv.at[z, j], to_z, p)

    def pass_in(j):
        rows = rows_of(j)
        return send(train.at[end, rows], train.at[end, rows], in_send.at[1, j], train_recv.at[end, j], across, p)

    def own_out(j):
        rows = rows_of(j)
        return send(t_ref.at[rows, outer], train.at[z, rows, outer], out_send.at[0, j], train_recv.at[z, j], end, p)

    def pass_out(j, block, k):
        part = train.at[block, rows_of(j), outer]
        return send(part, part, out_send.at[k, j], train_recv.at[block, j], end, p)

    def query_copy(to_z):
        return send(q_ref.at[:, inner], query_in, query_send.at[0], query_recv.at[0], to_z, p)

    def part_copy(j, half, block):
        rows = group_rows(j)
        return send(
            partial.at[half, block, rows], taken.at[p, half, rows],
            part_send.at[block, half, j], part_recv.at[p, half, j], z, block,
        )

    def part_wait(j, half, peer):
        dst = taken.at[peer, half, group_rows(j)]
        send(dst, dst, part_send.at[0, half, j], part_recv.at[peer, half, j], z, peer).wait_recv()

    def sums_copy(j, to_z):
        rows = group_rows(j)
        return send(sums.at[rows], sums_taken.at[rows], sums_send.at[j], sums_recv.at[j], to_z, p)

    def loop(body, low=0, high=chunks):
        def step(j, carry):
            body(j)
            return carry
        lax.fori_loop(low, high, step, 0)

    def multiply(first, number, half, blocks, columns, by_high, by_low):
        rows = pl.ds(pl.multiple_of(first, number), number)
        result = product(
            jnp.concatenate([train[block, rows, columns] for block in blocks], axis=0), by_high, by_low
        )
        for k, block in enumerate(blocks):
            partial[half, block, rows] = result[k * number:(k + 1) * number]

    def send_parts(s, half, block):
        @pl.when(p != block)
        def _():
            part_copy(s, half, block).start()

    def reduced(s, half):
        rows = group_rows(s)
        total = partial[half, p, rows]
        for step in range(1, 4):
            peer = lax.rem(p + step, 4)
            part_wait(s, half, peer)
            total = total + taken[peer, half, rows]
        return total

    def split_query(src, into_high, into_low):
        size = 128
        def step(k):
            some = pl.ds(pl.multiple_of(k * size, size), size)
            into_high[:, some], into_low[:, some] = split(src[some].T)
        loop(step, 0, queries // size)

    own_train = pltpu.make_async_copy(t_ref, train.at[z], local_sem.at[0])
    own_query = pltpu.make_async_copy(q_ref, query, local_sem.at[1])
    own_train.start()
    own_query.start()

    barrier = pltpu.get_barrier_semaphore()
    for step in range(1, 4):
        pl.semaphore_signal(barrier, inc=1, device_id=(g, z, lax.rem(p + step, 4)), device_id_type=MESH)

    @pl.when(is_end)
    def _():
        pl.semaphore_signal(barrier, inc=1, device_id=(g, beside, p), device_id_type=MESH)
        pl.semaphore_wait(barrier, 4)

    @pl.when(is_mid)
    def _():
        pl.semaphore_signal(barrier, inc=1, device_id=(g, across, p), device_id_type=MESH)
        pl.semaphore_signal(barrier, inc=1, device_id=(g, end, p), device_id_type=MESH)
        pl.semaphore_wait(barrier, 5)

    @pl.when(is_end)
    def _():
        query_copy(beside).start()
        loop(lambda j: own_in(j, beside).start())

    @pl.when(is_mid)
    def _():
        def begin(j):
            own_in(j, across).start()
            own_out(j).start()
        loop(begin)

    own_train.wait()
    own_query.wait()
    split_query(query, high, low)
    all_rows = t_ref.shape[0]
    per = chunks // groups
    size = all_rows // groups

    def send_all(half, block):
        loop(lambda s: send_parts(s, half, block), 0, groups)

    @pl.when(is_mid)
    def _():
        def wait_train(j, block):
            part = train.at[block, rows_of(j)]
            send(part, part, in_send.at[0, j], train_recv.at[block, j], across, p).wait_recv()

        def take_across(s):
            for k in range(per):
                wait_train(s * per + k, across)
                pass_out(s * per + k, across, 1).start()

        def take_end(s):
            for k in range(per):
                wait_train(s * per + k, end)
                pass_in(s * per + k).start()

        def take_far(s):
            for k in range(per):
                wait_train(s * per + k, far)
                pass_out(s * per + k, far, 2).start()

        def whole(s, block):
            multiply(s * size, size, 0, (block,), slice(None), high[...], low[...])
            send_parts(s, 0, block)

        def inward_part(s, block):
            multiply(s * size, size, 1, (block,), slice(0, inward), high_in[...], low_in[...])
            send_parts(s, 1, block)

        multiply(0, all_rows, 0, (z,), slice(None), high[...], low[...])
        send_all(0, z)

        def early(s):
            @pl.when(s == groups - 1)
            def _():
                query_copy(end).wait_recv()
                split_query(query_in, high_in, low_in)

            take_across(s)

            @pl.when(s == groups - 1)
            def _():
                take_end(0)

            whole(s, across)
        loop(early, 0, groups)

        multiply(0, all_rows, 1, (1, 2), slice(0, inward), high_in[...], low_in[...])
        send_all(1, 1)
        send_all(1, 2)

        def finish(s):
            rows = group_rows(s)
            sums[rows] = reduced(s, 1)
            sums_copy(s, end).start()
            o_ref[rows] = reduced(s, 0)

        def late(s):
            @pl.when(s < groups - 1)
            def _():
                take_end(s + 1)

            def one(k):
                block = jnp.where(k == 0, end, far)

                @pl.when(k == 1)
                def _():
                    take_far(s)

                inward_part(s, block)
                whole(s, block)
            loop(one, 0, 2)

            @pl.when(s > 0)
            def _():
                finish(s - 1)
        loop(late, 0, groups)
        finish(groups - 1)

        def drain(j):
            own_in(j, across).wait_send()
            pass_in(j).wait_send()
            own_out(j).wait_send()
            pass_out(j, across, 1).wait_send()
            pass_out(j, far, 2).wait_send()
        loop(drain)

        def drain_parts(s):
            sums_copy(s, end).wait_send()
            for half in (0, 1):
                for block in range(4):
                    @pl.when(p != block)
                    def _():
                        part_copy(s, half, block).wait_send()
        loop(drain_parts, 0, groups)

    @pl.when(is_end)
    def _():
        columns = slice(inward, depth)

        def wait_train(s, block):
            for k in range(per):
                part = train.at[block, rows_of(s * per + k), outer]
                send(part, part, in_send.at[0, 0], train_recv.at[block, s * per + k], beside, p).wait_recv()

        multiply(0, all_rows, 0, (z,), columns, high[inward:], low[inward:])
        send_all(0, z)

        def early(s):
            wait_train(s, 1)
            wait_train(s, 2)
            multiply(s * size, size, 0, (1, 2), columns, high[inward:], low[inward:])
            send_parts(s, 0, 1)
            send_parts(s, 0, 2)
        loop(early, 0, groups)

        def late(s):
            wait_train(s, across)
            multiply(s * size, size, 0, (across,), columns, high[inward:], low[inward:])
            send_parts(s, 0, across)
        loop(late, 0, groups)

        def finish(s):
            rows = group_rows(s)
            o_ref[rows] = reduced(s, 0)
        loop(finish, 0, groups)

        def add_sums(s):
            rows = group_rows(s)
            sums_copy(s, beside).wait_recv()
            o_ref[rows] = o_ref[rows] + sums_taken[rows]
        loop(add_sums, 0, groups)

        query_copy(beside).wait_send()
        loop(lambda j: own_in(j, beside).wait_send())

        def drain_parts(s):
            for block in range(4):
                @pl.when(p != block)
                def _():
                    part_copy(s, 0, block).wait_send()
        loop(drain_parts, 0, groups)


def line_of_four(query_feats, train_feats, out_weight):
    queries, depth = query_feats.shape
    rows = train_feats.shape[0]
    inward = min(INWARD, depth // 2)
    f32, bf16 = jnp.float32, jnp.bfloat16
    dma = pltpu.SemaphoreType.DMA
    sums = pl.pallas_call(
        functools.partial(kernel, inward, CHUNKS, GROUPS),
        out_shape=jax.ShapeDtypeStruct((rows, queries), f32),
        in_specs=[pl.BlockSpec(memory_space=pl.ANY)] * 2,
        out_specs=pl.BlockSpec(memory_space=pltpu.VMEM),
        scratch_shapes=[
            pltpu.VMEM((4, rows, depth), f32),
            pltpu.VMEM((queries, depth), f32),
            pltpu.VMEM((queries, inward), f32),
            pltpu.VMEM((depth, queries), bf16),
            pltpu.VMEM((depth, queries), bf16),
            pltpu.VMEM((inward, queries), bf16),
            pltpu.VMEM((inward, queries), bf16),
            pltpu.VMEM((2, 4, rows, queries), f32),
            pltpu.VMEM((4, 2, rows, queries), f32),
            pltpu.VMEM((rows, queries), f32),
            pltpu.VMEM((rows, queries), f32),
            dma((2,)),
            dma((4, CHUNKS)),
            dma((1,)),
            dma((4, 2, GROUPS)),
            dma((GROUPS,)),
            dma((2, CHUNKS)),
            dma((3, CHUNKS)),
            dma((1,)),
            dma((4, 2, GROUPS)),
            dma((GROUPS,)),
        ],
        compiler_params=pltpu.CompilerParams(
            collective_id=0, has_side_effects=True, vmem_limit_bytes=56 << 20
        ),
        cost_estimate=pl.CostEstimate(
            flops=3 * 2 * 4 * rows * queries * depth, bytes_accessed=4 * (rows + queries) * depth, transcendentals=0
        ),
    )(query_feats, train_feats)
    return sums * out_weight[:, None]


def any_mesh(query_feats, train_feats, out_weight):
    terms = lax.dot_general(
        lax.all_gather(train_feats, "query", axis=0, tiled=True),
        query_feats,
        (((1,), (1,)), ((), ())),
        precision=lax.Precision.HIGHEST,
        preferred_element_type=jnp.float32,
    )
    return lax.psum_scatter(terms, "proj", scatter_dimension=0, tiled=True) * out_weight[:, None]


def solution(mesh):
    placed = (P(("groups", "query"), "proj"), P(("groups", "query"), "proj"), P(("groups", "proj")))
    body = line_of_four if mesh.shape["query"] == mesh.shape["proj"] == 4 else any_mesh
    return jax.shard_map(
        body, mesh=mesh, in_specs=placed, out_specs=P(("groups", "proj"), "query"), check_vma=False
    )
```
